32 devices in a mesh: cache: 4 (over y, core), dev: 8 (over z, x).
Axes of the slice: x: 2, y: 2, z: 4, core: 2. Of those that a mesh axis runs over, the one named last changes fastest.
Arguments:
- queries: bfloat16 [4, 1024, 8192], P('cache', None, 'dev'), may hold values from -8 to 8
- store_kv: bfloat16 [128, 512, 2048], P('cache', 'dev'), may hold values from -4 to 4
- self_kv: bfloat16 [4, 1024, 2048], P('cache'), may hold values from -5 to 5
- rec_states: bfloat16 [4, 512, 8192], P('cache', None, 'dev'), may hold values from -400 to 400
- norm_gain: bfloat16 [8192], P('dev'), may hold values from 0.099609375 to 1.8984375
- w_kv: bfloat16 [8192, 2048], P('dev'), may hold values from -0.0625 to 0.0625
- retrieval: int32 [4, 16], replicated, may hold values from 0 to 127, as said below
- doc_home: int32 [128], replicated, may hold values from 0 to 127, as said below
- rec_index: int32 [4, 16, 32], P('cache'), may hold values from 0 to 511, as said below
Outputs:
- attended: bfloat16 [4, 1024, 8192], P('cache', None, 'dev')
The draws below stay inside these ranges and needn't reach their ends.
Inputs may be any that keep to these rules, and one draw needn't show every extreme that they name: `retrieval`: each request names 16 distinct documents; their store rows lie in exactly 4 of the groups of 32 consecutive rows, 4 in each. `doc_home`: every store row holds exactly one document. `rec_index`: the 32 positions of one block are distinct.
All inputs are finite; a program needn't handle non-finite values.
Results may differ from the reference program's by a relative error of at most 0.0045.
Values may be sent and summed in bfloat16 or wider, within the bound.
A program may use at most 128 MiB of HBM per device.

```python
import math
import jax
import jax.numpy as jnp
from jax import lax

D = 8192
QH = 64
KVH = 8
HD = 128
BLK = 512
RET = 16
CAP = 4
REC = 32
QLEN = 1024
DOC_GRP = 32
REQ = 4
DOCS = 128


def draw_queries(key, part):
    shape = (REQ, QLEN, QH * HD)
    base = 2.5 * jnp.clip(jax.random.normal(jax.random.fold_in(key, 1), shape, jnp.float32), -3.2, 3.2)
    return base.astype(jnp.bfloat16)


def draw_store_kv(key, part):
    shape = (DOCS, BLK, 2 * KVH * HD)
    base = jnp.clip(jax.random.normal(jax.random.fold_in(key, 2), shape, jnp.float32), -4.0, 4.0)
    return base.astype(jnp.bfloat16)


def draw_rec_states(key, part):
    shape = (REQ, RET * REC, D)
    row_scale = 10.0 ** jax.random.uniform(jax.random.fold_in(key, 3), (REQ, RET * REC, 1), jnp.float32)
    columns = jnp.arange(D).astype(jnp.float32) / D
    col_scale = 10.0 ** (0.25 * columns + 0.75 * jax.random.uniform(jax.random.fold_in(key, 4), (D,), jnp.float32))
    base = jnp.clip(jax.random.normal(jax.random.fold_in(key, 6), shape, jnp.float32), -4.0, 4.0)
    return (base * row_scale * col_scale[None, None, :]).astype(jnp.bfloat16)


def placement_tables(key):
    anchor = jax.random.fold_in(key, 11)
    home = jax.random.permutation(jax.random.fold_in(anchor, 1), DOCS).astype(jnp.int32)
    resident = jnp.zeros((DOCS,), jnp.int32).at[home].set(jnp.arange(DOCS, dtype=jnp.int32))
    offsets = jnp.arange(REQ, dtype=jnp.int32)

    def one_request(which):
        request_key = jax.random.fold_in(anchor, 100 + which)
        priority = jax.random.permutation(jax.random.fold_in(request_key, 1), REQ).astype(jnp.int32)
        priority = jnp.where(offsets == REQ - 1, -2, jnp.where(offsets == REQ // 2, -1, priority))
        order = jnp.argsort(priority, stable=True).astype(jnp.int32)
        used_groups = (which + order[:RET // CAP]) % REQ

        def within_group(group_slot):
            return jax.random.permutation(jax.random.fold_in(request_key, 2 + group_slot), DOC_GRP)[:CAP]
        within = jax.vmap(within_group)(jnp.arange(RET // CAP))
        store_rows = (used_groups[:, None] * DOC_GRP + within).reshape(RET)
        shuffled = jax.random.permutation(jax.random.fold_in(request_key, 999), RET)
        return resident[store_rows[shuffled]]
    chosen = jax.vmap(one_request)(jnp.arange(REQ, dtype=jnp.int32))
    return (home, chosen.astype(jnp.int32))


def draw_retrieval(key, part):
    return placement_tables(key)[1]


def draw_doc_home(key, part):
    return placement_tables(key)[0]


def draw_rec_index(key, part):

    def one_block(which):
        return jax.random.permutation(jax.random.fold_in(key, 50 + which), BLK)[:REC]
    return jax.vmap(one_block)(jnp.arange(REQ * RET)).reshape(REQ, RET, REC).astype(jnp.int32)


def block_scale(stream_key, extent, split, smallest, high):
    def one(axis_at, shards_of):
        heights = jax.random.uniform(jax.random.fold_in(jax.random.fold_in(stream_key, 6), axis_at), (shards_of,), jnp.float32, smallest / len(split), high / len(split))
        return jnp.repeat(jnp.exp(heights), extent[axis_at] // shards_of).reshape((-1,) + (1,) * (len(extent) - axis_at - 1))

    level = one(*split[0])
    for cut in split[1:]:
        level = level * one(*cut)
    return level


def centred(own_key, extent, spread, reach, shards=(), kind=jnp.bfloat16):
    entries = jax.random.normal(own_key, extent, jnp.float32) * spread
    if len(shards) > 0:
        entries = block_scale(own_key, extent, shards, -0.22, 0.18) * entries
    return jnp.clip(entries, min=-reach, max=reach).astype(kind)


def setup_inputs(seed: int = 0) -> dict:
    keys = jax.random.split(jax.random.key(seed), 10)
    return {
        "queries": draw_queries(jax.random.fold_in(keys[9], 71), 0),
        "store_kv": draw_store_kv(jax.random.fold_in(keys[9], 71), 0),
        "self_kv": centred(keys[2], (REQ, QLEN, 2 * KVH * HD), 1.0, 5.0, ((0, 4),)),
        "rec_states": draw_rec_states(jax.random.fold_in(keys[9], 71), 0),
        "norm_gain": jnp.clip(1.0 + 0.18 * jax.random.normal(keys[4], (D,), jnp.float32), 0.099609375, 1.8984375).astype(jnp.bfloat16),
        "w_kv": centred(keys[5], (D, 2 * KVH * HD), D ** -0.5, 0.0625, ((0, 8),)),
        "retrieval": draw_retrieval(jax.random.fold_in(keys[9], 71), 0),
        "doc_home": draw_doc_home(jax.random.fold_in(keys[9], 71), 0),
        "rec_index": draw_rec_index(jax.random.fold_in(keys[9], 71), 0),
    }


eps_norm = 1e-05

def head_columns(matrix, first_col):
    return lax.dynamic_slice_in_dim(matrix, first_col, HD, 1)

def reference(queries, store_kv, self_kv, rec_states, norm_gain, w_kv, retrieval, doc_home, rec_index):
    kv_width = KVH * HD
    ratio_heads = QH // KVH
    inv_root = 1.0 / math.sqrt(HD)
    visible = jnp.arange(QLEN, dtype=jnp.int32)[None, :] <= jnp.arange(QLEN, dtype=jnp.int32)[:, None]

    def one_request(request):
        wanted = lax.dynamic_index_in_dim(retrieval, request, 0, keepdims=False)
        stored_rows = jnp.take(doc_home, wanted, axis=0)
        fetched = jnp.take(store_kv, stored_rows, axis=0)
        states = lax.dynamic_index_in_dim(rec_states, request, 0, keepdims=False).astype(jnp.float32)
        mean_sq = lax.optimization_barrier(jnp.sum(states * states, axis=1)) / D
        normed = (states * norm_gain.astype(jnp.float32)[None, :] * lax.rsqrt(mean_sq + eps_norm)[:, None]).astype(jnp.bfloat16)
        redone = jnp.dot(normed, w_kv, preferred_element_type=jnp.float32).astype(jnp.bfloat16)
        redone = redone.reshape(RET, REC, 2 * kv_width)
        positions = lax.dynamic_index_in_dim(rec_index, request, 0, keepdims=False)
        onehot = positions[:, :, None] == jnp.arange(BLK, dtype=jnp.int32)[None, None, :]
        placed = jnp.einsum('kib,kic->kbc', onehot.astype(jnp.float32), redone.astype(jnp.float32), precision=lax.Precision.HIGHEST).astype(jnp.bfloat16)
        blocks = jnp.where(jnp.any(onehot, axis=1)[:, :, None], placed, fetched)
        flat_blocks = blocks.reshape(RET * BLK, 2 * kv_width)
        own_self = lax.dynamic_index_in_dim(self_kv, request, 0, keepdims=False)
        own_queries = lax.dynamic_index_in_dim(queries, request, 0, keepdims=False)

        def one_head(head_at):
            kv_head = head_at // ratio_heads
            query_rows = head_columns(own_queries, head_at * HD)
            doc_keys = head_columns(flat_blocks, kv_head * HD)
            doc_values = head_columns(flat_blocks, (KVH + kv_head) * HD)
            self_keys = head_columns(own_self, kv_head * HD)
            self_values = head_columns(own_self, (KVH + kv_head) * HD)
            doc_scores = jnp.dot(query_rows, doc_keys.T, preferred_element_type=jnp.float32) * inv_root
            self_scores = jnp.dot(query_rows, self_keys.T, preferred_element_type=jnp.float32) * inv_root
            self_scores = jnp.where(visible, self_scores, -jnp.inf)
            top = jnp.maximum(lax.optimization_barrier(jnp.max(doc_scores, axis=1)), lax.optimization_barrier(jnp.max(self_scores, axis=1)))
            doc_expd = jnp.exp(doc_scores - top[:, None])
            self_expd = jnp.exp(self_scores - top[:, None])
            total = lax.optimization_barrier(jnp.sum(doc_expd, axis=1)) + lax.optimization_barrier(jnp.sum(self_expd, axis=1))
            weighted = jnp.dot(doc_expd.astype(jnp.bfloat16), doc_values, preferred_element_type=jnp.float32)
            weighted = weighted + jnp.dot(self_expd.astype(jnp.bfloat16), self_values, preferred_element_type=jnp.float32)
            return (weighted / total[:, None]).astype(jnp.bfloat16)
        per_head = lax.map(one_head, jnp.arange(QH, dtype=jnp.int32))
        return jnp.transpose(per_head, (1, 0, 2)).reshape(QLEN, QH * HD)
    return lax.map(one_request, jnp.arange(REQ, dtype=jnp.int32))
```

```python
import functools
import math

import jax
import jax.numpy as jnp
from jax import lax
from jax.experimental import pallas as pl
from jax.experimental.pallas import tpu as pltpu
from jax.sharding import PartitionSpec as P

D = 8192
QH = 64
KVH = 8
HD = 128
RET = 16
CAP = 4
REC = 32
DOC_GRP = 32

eps_norm = 1e-05
MESH = pl.DeviceIdType.MESH
TQ = 256
REMOTE = True


def flip(index, bits, count):
    out = 0
    step = 1
    while step < count:
        digit = index // step % 2
        if bits // step % 2:
            digit = 1 - digit
        out = out + digit * step
        step *= 2
    return out


def gather_kernel(rows_ref, store_ref, out_ref):
    for head in range(KVH):
        out_ref[head, 0, :, :HD] = store_ref[0, :, head * HD : (head + 1) * HD]
        out_ref[head, 0, :, HD:] = store_ref[0, :, (KVH + head) * HD : (KVH + head + 1) * HD]


def gather_blocks(pick_row, store_kv, groups):
    tok, width = store_kv.shape[1:]
    return pl.pallas_call(
        gather_kernel,
        grid_spec=pltpu.PrefetchScalarGridSpec(
            num_scalar_prefetch=1,
            grid=(groups * CAP,),
            in_specs=[pl.BlockSpec((1, tok, width), lambda i, rows: (rows[i], 0, 0))],
            out_specs=pl.BlockSpec(
                (KVH, 1, tok, 2 * HD), lambda i, rows: (0, i // CAP, i % CAP, 0)
            ),
        ),
        out_shape=jax.ShapeDtypeStruct((KVH, groups, CAP * tok, 2 * HD), store_kv.dtype),
    )(pick_row, store_kv)


def nt(a, b):
    return lax.dot_general(a, b, (((1,), (1,)), ((), ())), preferred_element_type=jnp.float32)


def split_queries(q_ref, q2_ref, heads, prompt):
    scale = math.log2(math.e) / math.sqrt(HD)
    for head in range(heads):
        scaled = q_ref[:, head * HD : (head + 1) * HD].astype(jnp.float32) * scale
        high = scaled.astype(jnp.bfloat16)
        low = (scaled - high.astype(jnp.float32)).astype(jnp.bfloat16)
        q2_ref[head * prompt : (head + 1) * prompt, :HD] = high
        q2_ref[head * prompt : (head + 1) * prompt, HD:] = low


def self_pass(q2_ref, self_ref, k2_ref, v2_ref, acc_ref, top_ref, heads, prompt):
    keys = self_ref[:, :HD]
    k2_ref[:prompt, :HD] = keys
    k2_ref[:prompt, HD:] = keys
    v2_ref[:prompt, :HD] = self_ref[:, HD:]
    v2_ref[:prompt, HD:] = jnp.ones((prompt, HD), jnp.bfloat16)

    @pl.loop(0, heads)
    def _(head):
        for tile in range(prompt // TQ):
            width = (tile + 1) * TQ
            rows = pl.ds(pl.multiple_of(head * prompt + tile * TQ, TQ), TQ)
            scores = nt(q2_ref[rows, :], k2_ref[:width, :])
            at = lax.broadcasted_iota(jnp.int32, (TQ, width), 0) + tile * TQ
            key = lax.broadcasted_iota(jnp.int32, (TQ, width), 1)
            scores = jnp.where(key <= at, scores, -jnp.inf)
            top = jnp.max(scores, axis=1, keepdims=True)
            expd = jnp.exp2(scores - top).astype(jnp.bfloat16)
            acc_ref[rows, :] = jnp.dot(
                expd, v2_ref[:width, :], preferred_element_type=jnp.float32
            )
            top_ref[rows, :] = jnp.broadcast_to(top, (TQ, HD))


def block_pass(q2_ref, k2_ref, v2_ref, acc_ref, top_ref, rows_total, count, unroll=2):
    @pl.loop(0, rows_total // (TQ * unroll))
    def _(step):
        spans = [
            pl.ds(pl.multiple_of(step * (TQ * unroll) + part * TQ, TQ), TQ)
            for part in range(unroll)
        ]
        scores = [nt(q2_ref[rows, :], k2_ref[:count, :]) for rows in spans]
        for rows, score in zip(spans, scores):
            before = top_ref[rows, :]
            top = jnp.maximum(before, jnp.max(score, axis=1, keepdims=True))
            expd = jnp.exp2(score - top[:, :1]).astype(jnp.bfloat16)
            fade = jnp.exp2(before - top)
            fresh = jnp.dot(expd, v2_ref[:count, :], preferred_element_type=jnp.float32)
            acc_ref[rows, :HD] = acc_ref[rows, :HD] * fade + fresh[:, :HD]
            acc_ref[rows, HD:] = acc_ref[rows, HD:] * fade + fresh[:, HD:]
            top_ref[rows, :] = top


def neutral(kv, keep, first_key, k2_ref, v2_ref, base):
    count = kv.shape[0]
    keys = kv[:, :HD] * keep + first_key * (1 - keep)
    k2_ref[base : base + count, :HD] = keys
    k2_ref[base : base + count, HD:] = keys
    v2_ref[base : base + count, :HD] = kv[:, HD:] * keep
    v2_ref[base : base + count, HD:] = keep


def finish(acc_ref, out_ref, heads, prompt):
    @pl.loop(0, prompt // TQ)
    def _(tile):
        rows = pl.ds(pl.multiple_of(tile * TQ, TQ), TQ)
        for head in range(heads):
            part = pl.ds(pl.multiple_of(head * prompt + tile * TQ, TQ), TQ)
            out_ref[rows, head * HD : (head + 1) * HD] = (
                acc_ref[part, :HD] / acc_ref[part, HD:]
            ).astype(out_ref.dtype)


def plain_kernel(heads, prompt, chunk, q_ref, self_ref, kv_ref, keep_ref, rec_ref, out_ref,
                 q2_ref, k2_ref, v2_ref, acc_ref, top_ref):
    split_queries(q_ref, q2_ref, heads, prompt)
    self_pass(q2_ref, self_ref, k2_ref, v2_ref, acc_ref, top_ref, heads, prompt)
    first_key = self_ref[0:1, :HD]

    @pl.loop(0, kv_ref.shape[0] // chunk)
    def _(at):
        rows = pl.ds(pl.multiple_of(at * chunk, chunk), chunk)
        neutral(kv_ref[rows, :], keep_ref[rows, :], first_key, k2_ref, v2_ref, 0)
        block_pass(q2_ref, k2_ref, v2_ref, acc_ref, top_ref, heads * prompt, chunk)

    count = rec_ref.shape[0]
    neutral(rec_ref[...], jnp.ones((count, HD), jnp.bfloat16), first_key, k2_ref, v2_ref, 0)
    block_pass(q2_ref, k2_ref, v2_ref, acc_ref, top_ref, heads * prompt, count)
    finish(acc_ref, out_ref, heads, prompt)


def state_scratch(rows, chunk):
    return [
        pltpu.VMEM((rows, 2 * HD), jnp.bfloat16),
        pltpu.VMEM((chunk, 2 * HD), jnp.bfloat16),
        pltpu.VMEM((chunk, 2 * HD), jnp.bfloat16),
        pltpu.VMEM((rows, 2 * HD), jnp.float32),
        pltpu.VMEM((rows, HD), jnp.float32),
    ]


def plain_attention(q, own_self, kv, keep, rec):
    prompt, width = q.shape
    heads = width // HD
    chunk = min(2048, kv.shape[0])
    vmem = pl.BlockSpec(memory_space=pltpu.VMEM)
    return pl.pallas_call(
        functools.partial(plain_kernel, heads, prompt, chunk),
        out_shape=jax.ShapeDtypeStruct((prompt, width), jnp.bfloat16),
        in_specs=[vmem] * 5,
        out_specs=vmem,
        scratch_shapes=state_scratch(heads * prompt, chunk),
        compiler_params=pltpu.CompilerParams(vmem_limit_bytes=60 * 1024 * 1024),
    )(q, own_self, kv, keep, rec)


def remote_kernel(heads, prompt, groups, members, q_ref, self_ref, keep_ref, x_ref, sq_ref, w_ref,
                  sent_ref, out_ref, q2_ref, k2_ref, v2_ref, acc_ref, top_ref, kv_ref, part_ref,
                  near_ref, mid_ref, far_ref, sums_ref, kv_send, kv_recv, near_send, near_recv,
                  far_send, far_recv, sq_send, sq_recv, local_sem):
    my_group = lax.axis_index("cache")
    me = lax.axis_index("dev")
    rec_rows = x_ref.shape[0]
    half = members // 2
    own = pltpu.make_async_copy(sent_ref.at[me, my_group], kv_ref.at[0, 0], local_sem)
    own.start()

    barrier = pltpu.get_barrier_semaphore()
    for k in range(members):
        for j in range(groups):
            if k or j:
                pl.semaphore_signal(
                    barrier, inc=1,
                    device_id={"cache": flip(my_group, j, groups), "dev": flip(me, k, members)},
                    device_id_type=MESH,
                )

    @pl.loop(0, members)
    def _(head):
        for side in range(2):
            cols = pl.ds(pl.multiple_of((side * KVH + head) * HD, HD), HD)
            part_ref[head, :, side * HD : (side + 1) * HD] = jnp.dot(
                x_ref[...], w_ref[:, cols], preferred_element_type=jnp.float32
            ).astype(jnp.bfloat16)

    pl.semaphore_wait(barrier, members * groups - 1)

    def kv_copy(k, j):
        to_group, to = flip(my_group, j, groups), flip(me, k, members)
        return pltpu.make_async_remote_copy(
            src_ref=sent_ref.at[to, to_group], dst_ref=kv_ref.at[k, j],
            send_sem=kv_send.at[k, j], recv_sem=kv_recv.at[k, j],
            device_id={"cache": to_group, "dev": to}, device_id_type=MESH,
        )

    def near_copy(a, which):
        to = flip(me, a, members)
        return pltpu.make_async_remote_copy(
            src_ref=part_ref.at[flip(to, half * which, members)], dst_ref=near_ref.at[a - 1, which],
            send_sem=near_send.at[a - 1, which], recv_sem=near_recv.at[a - 1, which],
            device_id={"cache": my_group, "dev": to}, device_id_type=MESH,
        )

    def sq_copy(k):
        return pltpu.make_async_remote_copy(
            src_ref=sq_ref, dst_ref=sums_ref.at[k - 1],
            send_sem=sq_send.at[k - 1], recv_sem=sq_recv.at[k - 1],
            device_id={"cache": my_group, "dev": flip(me, k, members)}, device_id_type=MESH,
        )

    for k in (4, 0, 1, 6):
        for j in range(groups):
            if k or j:
                kv_copy(k, j).start()
    for a in range(1, half):
        near_copy(a, 1).start()
    for k in (2, 5, 3, 7):
        for j in range(groups):
            kv_copy(k, j).start()
    for a in range(1, half):
        near_copy(a, 0).start()
    for k in range(1, members):
        sq_copy(k).start()

    split_queries(q_ref, q2_ref, heads, prompt)
    self_pass(q2_ref, self_ref, k2_ref, v2_ref, acc_ref, top_ref, heads, prompt)
    first_key = self_ref[0:1, :HD]
    far = pltpu.make_async_remote_copy(
        src_ref=mid_ref, dst_ref=far_ref, send_sem=far_send, recv_sem=far_recv,
        device_id={"cache": my_group, "dev": flip(me, half, members)}, device_id_type=MESH,
    )
    size = kv_ref.shape[2]
    for pair in range(members // 2):
        for k in (2 * pair, 2 * pair + 1):
            source = flip(me, k, members)
            for j in range(groups):
                if k or j:
                    kv_copy(k, j).wait_recv()
                else:
                    own.wait()
                place = flip(my_group, j, groups)
                neutral(
                    kv_ref[k, j], keep_ref[source, place], first_key, k2_ref, v2_ref,
                    ((k % 2) * groups + j) * size,
                )
        block_pass(q2_ref, k2_ref, v2_ref, acc_ref, top_ref, heads * prompt, 2 * groups * size)
        if pair == 1:
            total = part_ref[flip(me, half, members)].astype(jnp.float32)
            for a in range(1, half):
                near_copy(a, 1).wait_recv()
                total = total + near_ref[a - 1, 1].astype(jnp.float32)
            mid_ref[...] = total.astype(jnp.bfloat16)
            far.start()

    square = sq_ref[...]
    for k in range(1, members):
        sq_copy(k).wait_recv()
        square = square + sums_ref[k - 1]
    inv_rms = jnp.transpose(lax.rsqrt(square / D + eps_norm))[:, :1]
    total = part_ref[me].astype(jnp.float32)
    for a in range(1, half):
        near_copy(a, 0).wait_recv()
        total = total + near_ref[a - 1, 0].astype(jnp.float32)
    far.wait_recv()
    redone = ((total + far_ref[...].astype(jnp.float32)) * inv_rms).astype(jnp.bfloat16)
    neutral(redone, jnp.ones((rec_rows, HD), jnp.bfloat16), first_key, k2_ref, v2_ref, 0)
    block_pass(q2_ref, k2_ref, v2_ref, acc_ref, top_ref, heads * prompt, rec_rows)
    finish(acc_ref, out_ref, heads, prompt)

    for k in range(members):
        for j in range(groups):
            if k or j:
                kv_copy(k, j).wait_send()
    for a in range(1, half):
        near_copy(a, 0).wait_send()
        near_copy(a, 1).wait_send()
    for k in range(1, members):
        sq_copy(k).wait_send()
    far.wait_send()


def remote_attention(q, own_self, keep, x, squares, w, sent):
    prompt, width = q.shape
    heads = width // HD
    members, groups = keep.shape[:2]
    size = sent.shape[2]
    rec_rows = x.shape[0]
    half = members // 2
    vmem = pl.BlockSpec(memory_space=pltpu.VMEM)
    dma = pltpu.SemaphoreType.DMA
    block = (rec_rows, 2 * HD)
    return pl.pallas_call(
        functools.partial(remote_kernel, heads, prompt, groups, members),
        out_shape=jax.ShapeDtypeStruct((prompt, width), jnp.bfloat16),
        in_specs=[vmem] * 6 + [pl.BlockSpec(memory_space=pl.ANY)],
        out_specs=vmem,
        scratch_shapes=state_scratch(heads * prompt, 2 * groups * size) + [
            pltpu.VMEM((members, groups, size, 2 * HD), jnp.bfloat16),
            pltpu.VMEM((members,) + block, jnp.bfloat16),
            pltpu.VMEM((half - 1, 2) + block, jnp.bfloat16),
            pltpu.VMEM(block, jnp.bfloat16),
            pltpu.VMEM(block, jnp.bfloat16),
            pltpu.VMEM((members - 1,) + squares.shape, jnp.float32),
            dma((members, groups)), dma((members, groups)),
            dma((half - 1, 2)), dma((half - 1, 2)), dma, dma,
            dma((members - 1,)), dma((members - 1,)), dma,
        ],
        compiler_params=pltpu.CompilerParams(
            vmem_limit_bytes=61 * 1024 * 1024, collective_id=0, has_side_effects=True
        ),
    )(q, own_self, keep, x, squares, w, sent)


def shards(queries, store_kv, self_kv, rec_states, norm_gain, w_kv, retrieval, doc_home, rec_index):
    groups = lax.axis_size("cache")
    members = lax.axis_size("dev")
    my_group = lax.axis_index("cache")
    my_member = lax.axis_index("dev")
    per_device = QH // members
    my_head = my_member * per_device // (QH // KVH)
    tok, kv_width = store_kv.shape[1:]
    spots = groups * CAP

    docs = jnp.arange(doc_home.shape[0], dtype=jnp.int32)
    stored_at = jnp.sum(
        jnp.where(retrieval[:, :, None] == docs, doc_home[None, None, :], 0), axis=2
    )
    source = stored_at // DOC_GRP
    before = jnp.arange(RET)[None, :] < jnp.arange(RET)[:, None]
    same_home = source[:, :, None] == source[:, None, :]
    rank = jnp.sum((same_home & before[None]).astype(jnp.int32), axis=2)
    places = jnp.arange(CAP, dtype=jnp.int32)
    mine = (source[:, None, :] == my_group) & (rank[:, None, :] == places[None, :, None])
    pick_row = jnp.sum(jnp.where(mine, (stored_at % DOC_GRP)[:, None, :], 0), axis=2)
    sent = gather_blocks(pick_row.reshape(-1), store_kv, groups)

    spot = lax.dynamic_index_in_dim(source * CAP + rank, my_group, 0, keepdims=False)
    held = spot[None, :] == jnp.arange(spots, dtype=jnp.int32)[:, None]
    full = tok * members
    fresh = jnp.all(rec_index[0][:, :, None] != jnp.arange(full, dtype=jnp.int32), axis=1)
    keep = jnp.any(held[:, :, None] & fresh[None], axis=1)
    keep = jnp.transpose(keep.reshape(groups, CAP, members, tok), (2, 0, 1, 3))
    keep = jnp.broadcast_to(
        keep.reshape(members, groups, CAP * tok, 1).astype(jnp.bfloat16),
        (members, groups, CAP * tok, HD),
    )

    own_self = jnp.concatenate(
        [
            lax.dynamic_slice_in_dim(self_kv[0], my_head * HD, HD, 1),
            lax.dynamic_slice_in_dim(self_kv[0], (KVH + my_head) * HD, HD, 1),
        ],
        axis=1,
    )
    states = rec_states[0].astype(jnp.float32)
    squares = jnp.sum(states * states, axis=1)
    if REMOTE and members == KVH and groups * CAP == RET:
        x = (states * norm_gain.astype(jnp.float32)[None, :]).astype(jnp.bfloat16)
        wide = jnp.broadcast_to(squares[None, :], (8, squares.shape[0]))
        return remote_attention(queries[0], own_self, keep, x, wide, w_kv, sent)[None]

    inv_rms = lax.rsqrt(lax.psum(squares, "dev") / D + eps_norm)
    x = (states * norm_gain.astype(jnp.float32)[None, :] * inv_rms[:, None]).astype(jnp.bfloat16)
    summed = lax.psum(jnp.dot(x, w_kv, preferred_element_type=jnp.float32), "dev")
    redone = jnp.concatenate(
        [
            lax.dynamic_slice_in_dim(summed, my_head * HD, HD, 1),
            lax.dynamic_slice_in_dim(summed, (KVH + my_head) * HD, HD, 1),
        ],
        axis=1,
    ).astype(jnp.bfloat16)
    arrived = lax.all_to_all(sent, "cache", split_axis=1, concat_axis=1, tiled=True)
    arrived = jnp.repeat(arrived, members // KVH, axis=0)
    arrived = lax.all_to_all(arrived, "dev", split_axis=0, concat_axis=0, tiled=True)
    out = plain_attention(
        queries[0], own_self, arrived.reshape(-1, 2 * HD), keep.reshape(-1, HD), redone
    )
    return out[None]


def solution(mesh):
    placed = (
        P("cache", None, "dev"),
        P("cache", "dev", None),
        P("cache", None, None),
        P("cache", None, "dev"),
        P("dev"),
        P("dev", None),
        P(),
        P(),
        P("cache", None, None),
    )
    return jax.shard_map(
        shards, mesh=mesh, in_specs=placed, out_specs=P("cache", None, "dev"), check_vma=False
    )
```

```python
import functools
import math

import jax
import jax.numpy as jnp
from jax import lax
from jax.experimental import pallas as pl
from jax.experimental.pallas import tpu as pltpu
from jax.sharding import PartitionSpec as P

D = 8192
QH = 64
KVH = 8
HD = 128
RET = 16
CAP = 4
REC = 32
DOC_GRP = 32

eps_norm = 1e-05
MESH = pl.DeviceIdType.MESH
TQ = 256
REMOTE = True


def flip(index, bits, count):
    out = 0
    step = 1
    while step < count:
        digit = index // step % 2
        if bits // step % 2:
            digit = 1 - digit
        out = out + digit * step
        step *= 2
    return out


def gather_kernel(rows_ref, *refs):
    out_ref = refs[-1]
    tok = refs[0].shape[1]
    for place, store_ref in enumerate(refs[:-1]):
        span = slice(place * tok, (place + 1) * tok)
        for head in range(KVH):
            out_ref[head, 0, span, :HD] = store_ref[0, :, head * HD : (head + 1) * HD]
            out_ref[head, 0, span, HD:] = store_ref[0, :, (KVH + head) * HD : (KVH + head + 1) * HD]


def gather_blocks(pick_row, store_kv, groups):
    tok, width = store_kv.shape[1:]

    def spec(place):
        return pl.BlockSpec((1, tok, width), lambda i, rows: (rows[i * CAP + place], 0, 0))

    return pl.pallas_call(
        gather_kernel,
        grid_spec=pltpu.PrefetchScalarGridSpec(
            num_scalar_prefetch=1,
            grid=(groups,),
            in_specs=[spec(place) for place in range(CAP)],
            out_specs=pl.BlockSpec((KVH, 1, CAP * tok, 2 * HD), lambda i, rows: (0, i, 0, 0)),
        ),
        out_shape=jax.ShapeDtypeStruct((KVH, groups, CAP * tok, 2 * HD), store_kv.dtype),
    )(pick_row, *[store_kv] * CAP)


def nt(a, b):
    return lax.dot_general(a, b, (((1,), (1,)), ((), ())), preferred_element_type=jnp.float32)


def split_queries(q_ref, q2_ref, heads, prompt):
    scale = math.log2(math.e) / math.sqrt(HD)
    for head in range(heads):
        scaled = q_ref[:, head * HD : (head + 1) * HD].astype(jnp.float32) * scale
        high = scaled.astype(jnp.bfloat16)
        low = (scaled - high.astype(jnp.float32)).astype(jnp.bfloat16)
        q2_ref[head * prompt : (head + 1) * prompt, :HD] = high
        q2_ref[head * prompt : (head + 1) * prompt, HD:] = low


def self_pass(q2_ref, self_ref, k2_ref, v2_ref, acc_ref, top_ref, heads, prompt):
    keys = self_ref[:, :HD]
    k2_ref[:prompt, :HD] = keys
    k2_ref[:prompt, HD:] = keys
    v2_ref[:prompt, :HD] = self_ref[:, HD:]
    v2_ref[:prompt, HD:] = jnp.ones((prompt, HD), jnp.bfloat16)

    @pl.loop(0, heads)
    def _(head):
        for tile in range(prompt // TQ):
            width = (tile + 1) * TQ
            rows = pl.ds(pl.multiple_of(head * prompt + tile * TQ, TQ), TQ)
            scores = nt(q2_ref[rows, :], k2_ref[:width, :])
            at = lax.broadcasted_iota(jnp.int32, (TQ, width), 0) + tile * TQ
            key = lax.broadcasted_iota(jnp.int32, (TQ, width), 1)
            scores = jnp.where(key <= at, scores, -jnp.inf)
            top = jnp.max(scores, axis=1, keepdims=True)
            expd = jnp.exp2(scores - top).astype(jnp.bfloat16)
            acc_ref[rows, :] = jnp.dot(
                expd, v2_ref[:width, :], preferred_element_type=jnp.float32
            )
            top_ref[rows, :] = jnp.broadcast_to(top, (TQ, HD))


def block_pass(q2_ref, k2_ref, v2_ref, acc_ref, top_ref, rows_total, count, unroll=4):
    @pl.loop(0, rows_total // (TQ * unroll))
    def _(step):
        spans = [
            pl.ds(pl.multiple_of(step * (TQ * unroll) + part * TQ, TQ), TQ)
            for part in range(unroll)
        ]
        scores = [nt(q2_ref[rows, :], k2_ref[:count, :]) for rows in spans]
        for rows, score in zip(spans, scores):
            before = top_ref[rows, :]
            top = jnp.maximum(before, jnp.max(score, axis=1, keepdims=True))
            expd = jnp.exp2(score - top[:, :1]).astype(jnp.bfloat16)
            fade = jnp.exp2(before - top)
            fresh = jnp.dot(expd, v2_ref[:count, :], preferred_element_type=jnp.float32)
            acc_ref[rows, :HD] = acc_ref[rows, :HD] * fade + fresh[:, :HD]
            acc_ref[rows, HD:] = acc_ref[rows, HD:] * fade + fresh[:, HD:]
            top_ref[rows, :] = top


def neutral(kv, keep, first_key, k2_ref, v2_ref, base):
    count = kv.shape[0]
    keys = kv[:, :HD] * keep + first_key * (1 - keep)
    k2_ref[base : base + count, :HD] = keys
    k2_ref[base : base + count, HD:] = keys
    v2_ref[base : base + count, :HD] = kv[:, HD:] * keep
    v2_ref[base : base + count, HD:] = keep


def finish(acc_ref, out_ref, heads, prompt):
    @pl.loop(0, prompt // TQ)
    def _(tile):
        rows = pl.ds(pl.multiple_of(tile * TQ, TQ), TQ)
        for head in range(heads):
            part = pl.ds(pl.multiple_of(head * prompt + tile * TQ, TQ), TQ)
            out_ref[rows, head * HD : (head + 1) * HD] = (
                acc_ref[part, :HD] / acc_ref[part, HD:]
            ).astype(out_ref.dtype)


def plain_kernel(heads, prompt, chunk, q_ref, self_ref, kv_ref, keep_ref, rec_ref, out_ref,
                 q2_ref, k2_ref, v2_ref, acc_ref, top_ref):
    split_queries(q_ref, q2_ref, heads, prompt)
    self_pass(q2_ref, self_ref, k2_ref, v2_ref, acc_ref, top_ref, heads, prompt)
    first_key = self_ref[0:1, :HD]

    @pl.loop(0, kv_ref.shape[0] // chunk)
    def _(at):
        rows = pl.ds(pl.multiple_of(at * chunk, chunk), chunk)
        neutral(kv_ref[rows, :], keep_ref[rows, :], first_key, k2_ref, v2_ref, 0)
        block_pass(q2_ref, k2_ref, v2_ref, acc_ref, top_ref, heads * prompt, chunk)

    count = rec_ref.shape[0]
    neutral(rec_ref[...], jnp.ones((count, HD), jnp.bfloat16), first_key, k2_ref, v2_ref, 0)
    block_pass(q2_ref, k2_ref, v2_ref, acc_ref, top_ref, heads * prompt, count)
    finish(acc_ref, out_ref, heads, prompt)


def state_scratch(rows, chunk):
    return [
        pltpu.VMEM((rows, 2 * HD), jnp.bfloat16),
        pltpu.VMEM((chunk, 2 * HD), jnp.bfloat16),
        pltpu.VMEM((chunk, 2 * HD), jnp.bfloat16),
        pltpu.VMEM((rows, 2 * HD), jnp.float32),
        pltpu.VMEM((rows, HD), jnp.float32),
    ]


def plain_attention(q, own_self, kv, keep, rec):
    prompt, width = q.shape
    heads = width // HD
    chunk = min(2048, kv.shape[0])
    vmem = pl.BlockSpec(memory_space=pltpu.VMEM)
    return pl.pallas_call(
        functools.partial(plain_kernel, heads, prompt, chunk),
        out_shape=jax.ShapeDtypeStruct((prompt, width), jnp.bfloat16),
        in_specs=[vmem] * 5,
        out_specs=vmem,
        scratch_shapes=state_scratch(heads * prompt, chunk),
        compiler_params=pltpu.CompilerParams(vmem_limit_bytes=60 * 1024 * 1024),
    )(q, own_self, kv, keep, rec)


def remote_kernel(heads, prompt, groups, members, q_ref, self_ref, keep_ref, x_ref, sq_ref, w_ref,
                  sent_ref, out_ref, q2_ref, k2_ref, v2_ref, acc_ref, top_ref, kv_ref, part_ref,
                  near_ref, mid_ref, far_ref, sums_ref, kv_send, kv_recv, near_send, near_recv,
                  far_send, far_recv, sq_send, sq_recv, local_sem):
    my_group = lax.axis_index("cache")
    me = lax.axis_index("dev")
    rec_rows = x_ref.shape[0]
    half = members // 2
    own = pltpu.make_async_copy(sent_ref.at[me, my_group], kv_ref.at[0, 0], local_sem)
    own.start()

    barrier = pltpu.get_barrier_semaphore()
    for k in range(members):
        for j in range(groups):
            if k or j:
                pl.semaphore_signal(
                    barrier, inc=1,
                    device_id={"cache": flip(my_group, j, groups), "dev": flip(me, k, members)},
                    device_id_type=MESH,
                )

    @pl.loop(0, members)
    def _(head):
        for side in range(2):
            cols = pl.ds(pl.multiple_of((side * KVH + head) * HD, HD), HD)
            part_ref[head, :, side * HD : (side + 1) * HD] = jnp.dot(
                x_ref[...], w_ref[:, cols], preferred_element_type=jnp.float32
            ).astype(jnp.bfloat16)

    pl.semaphore_wait(barrier, members * groups - 1)

    def kv_copy(k, j):
        to_group, to = flip(my_group, j, groups), flip(me, k, members)
        return pltpu.make_async_remote_copy(
            src_ref=sent_ref.at[to, to_group], dst_ref=kv_ref.at[k, j],
            send_sem=kv_send.at[k, j], recv_sem=kv_recv.at[k, j],
            device_id={"cache": to_group, "dev": to}, device_id_type=MESH,
        )

    def near_copy(a, which):
        to = flip(me, a, members)
        return pltpu.make_async_remote_copy(
            src_ref=part_ref.at[flip(to, half * which, members)], dst_ref=near_ref.at[a - 1, which],
            send_sem=near_send.at[a - 1, which], recv_sem=near_recv.at[a - 1, which],
            device_id={"cache": my_group, "dev": to}, device_id_type=MESH,
        )

    def sq_copy(k):
        return pltpu.make_async_remote_copy(
            src_ref=sq_ref, dst_ref=sums_ref.at[k - 1],
            send_sem=sq_send.at[k - 1], recv_sem=sq_recv.at[k - 1],
            device_id={"cache": my_group, "dev": flip(me, k, members)}, device_id_type=MESH,
        )

    for k in (4, 0, 1, 6):
        for j in range(groups):
            if k or j:
                kv_copy(k, j).start()
    for a in range(1, half):
        near_copy(a, 1).start()
    for k in (2, 5, 3, 7):
        for j in range(groups):
            kv_copy(k, j).start()
    for a in range(1, half):
        near_copy(a, 0).start()
    for k in range(1, members):
        sq_copy(k).start()

    split_queries(q_ref, q2_ref, heads, prompt)
    self_pass(q2_ref, self_ref, k2_ref, v2_ref, acc_ref, top_ref, heads, prompt)
    first_key = self_ref[0:1, :HD]
    far = pltpu.make_async_remote_copy(
        src_ref=mid_ref, dst_ref=far_ref, send_sem=far_send, recv_sem=far_recv,
        device_id={"cache": my_group, "dev": flip(me, half, members)}, device_id_type=MESH,
    )
    size = kv_ref.shape[2]
    for pair in range(members // 2):
        for k in (2 * pair, 2 * pair + 1):
            source = flip(me, k, members)
            for j in range(groups):
                if k or j:
                    kv_copy(k, j).wait_recv()
                else:
                    own.wait()
                place = flip(my_group, j, groups)
                neutral(
                    kv_ref[k, j], keep_ref[source, place], first_key, k2_ref, v2_ref,
                    ((k % 2) * groups + j) * size,
                )
        block_pass(q2_ref, k2_ref, v2_ref, acc_ref, top_ref, heads * prompt, 2 * groups * size)
        if pair == 1:
            total = part_ref[flip(me, half, members)].astype(jnp.float32)
            for a in range(1, half):
                near_copy(a, 1).wait_recv()
                total = total + near_ref[a - 1, 1].astype(jnp.float32)
            mid_ref[...] = total.astype(jnp.bfloat16)
            far.start()

    square = sq_ref[...]
    for k in range(1, members):
        sq_copy(k).wait_recv()
        square = square + sums_ref[k - 1]
    inv_rms = jnp.transpose(lax.rsqrt(square / D + eps_norm))[:, :1]
    total = part_ref[me].astype(jnp.float32)
    for a in range(1, half):
        near_copy(a, 0).wait_recv()
        total = total + near_ref[a - 1, 0].astype(jnp.float32)
    far.wait_recv()
    redone = ((total + far_ref[...].astype(jnp.float32)) * inv_rms).astype(jnp.bfloat16)
    neutral(redone, jnp.ones((rec_rows, HD), jnp.bfloat16), first_key, k2_ref, v2_ref, 0)
    block_pass(q2_ref, k2_ref, v2_ref, acc_ref, top_ref, heads * prompt, rec_rows)
    finish(acc_ref, out_ref, heads, prompt)

    for k in range(members):
        for j in range(groups):
            if k or j:
                kv_copy(k, j).wait_send()
    for a in range(1, half):
        near_copy(a, 0).wait_send()
        near_copy(a, 1).wait_send()
    for k in range(1, members):
        sq_copy(k).wait_send()
    far.wait_send()


def remote_attention(q, own_self, keep, x, squares, w, sent):
    prompt, width = q.shape
    heads = width // HD
    members, groups = keep.shape[:2]
    size = sent.shape[2]
    rec_rows = x.shape[0]
    half = members // 2
    vmem = pl.BlockSpec(memory_space=pltpu.VMEM)
    dma = pltpu.SemaphoreType.DMA
    block = (rec_rows, 2 * HD)
    return pl.pallas_call(
        functools.partial(remote_kernel, heads, prompt, groups, members),
        out_shape=jax.ShapeDtypeStruct((prompt, width), jnp.bfloat16),
        in_specs=[vmem] * 6 + [pl.BlockSpec(memory_space=pl.ANY)],
        out_specs=vmem,
        scratch_shapes=state_scratch(heads * prompt, 2 * groups * size) + [
            pltpu.VMEM((members, groups, size, 2 * HD), jnp.bfloat16),
            pltpu.VMEM((members,) + block, jnp.bfloat16),
            pltpu.VMEM((half - 1, 2) + block, jnp.bfloat16),
            pltpu.VMEM(block, jnp.bfloat16),
            pltpu.VMEM(block, jnp.bfloat16),
            pltpu.VMEM((members - 1,) + squares.shape, jnp.float32),
            dma((members, groups)), dma((members, groups)),
            dma((half - 1, 2)), dma((half - 1, 2)), dma, dma,
            dma((members - 1,)), dma((members - 1,)), dma,
        ],
        compiler_params=pltpu.CompilerParams(
            vmem_limit_bytes=61 * 1024 * 1024, collective_id=0, has_side_effects=True
        ),
    )(q, own_self, keep, x, squares, w, sent)


def shards(queries, store_kv, self_kv, rec_states, norm_gain, w_kv, retrieval, doc_home, rec_index):
    groups = lax.axis_size("cache")
    members = lax.axis_size("dev")
    my_group = lax.axis_index("cache")
    my_member = lax.axis_index("dev")
    per_device = QH // members
    my_head = my_member * per_device // (QH // KVH)
    tok, kv_width = store_kv.shape[1:]
    spots = groups * CAP

    docs = jnp.arange(doc_home.shape[0], dtype=jnp.int32)
    stored_at = jnp.sum(
        jnp.where(retrieval[:, :, None] == docs, doc_home[None, None, :], 0), axis=2
    )
    source = stored_at // DOC_GRP
    before = jnp.arange(RET)[None, :] < jnp.arange(RET)[:, None]
    same_home = source[:, :, None] == source[:, None, :]
    rank = jnp.sum((same_home & before[None]).astype(jnp.int32), axis=2)
    places = jnp.arange(CAP, dtype=jnp.int32)
    mine = (source[:, None, :] == my_group) & (rank[:, None, :] == places[None, :, None])
    pick_row = jnp.sum(jnp.where(mine, (stored_at % DOC_GRP)[:, None, :], 0), axis=2)
    sent = gather_blocks(pick_row.reshape(-1), store_kv, groups)

    spot = lax.dynamic_index_in_dim(source * CAP + rank, my_group, 0, keepdims=False)
    held = spot[None, :] == jnp.arange(spots, dtype=jnp.int32)[:, None]
    full = tok * members
    fresh = jnp.all(rec_index[0][:, :, None] != jnp.arange(full, dtype=jnp.int32), axis=1)
    keep = jnp.any(held[:, :, None] & fresh[None], axis=1)
    keep = jnp.transpose(keep.reshape(groups, CAP, members, tok), (2, 0, 1, 3))
    keep = jnp.broadcast_to(
        keep.reshape(members, groups, CAP * tok, 1).astype(jnp.bfloat16),
        (members, groups, CAP * tok, HD),
    )

    own_self = jnp.concatenate(
        [
            lax.dynamic_slice_in_dim(self_kv[0], my_head * HD, HD, 1),
            lax.dynamic_slice_in_dim(self_kv[0], (KVH + my_head) * HD, HD, 1),
        ],
        axis=1,
    )
    states = rec_states[0].astype(jnp.float32)
    squares = jnp.sum(states * states, axis=1)
    if REMOTE and members == KVH and groups * CAP == RET:
        x = (states * norm_gain.astype(jnp.float32)[None, :]).astype(jnp.bfloat16)
        wide = jnp.broadcast_to(squares[None, :], (8, squares.shape[0]))
        return remote_attention(queries[0], own_self, keep, x, wide, w_kv, sent)[None]

    inv_rms = lax.rsqrt(lax.psum(squares, "dev") / D + eps_norm)
    x = (states * norm_gain.astype(jnp.float32)[None, :] * inv_rms[:, None]).astype(jnp.bfloat16)
    summed = lax.psum(jnp.dot(x, w_kv, preferred_element_type=jnp.float32), "dev")
    redone = jnp.concatenate(
        [
            lax.dynamic_slice_in_dim(summed, my_head * HD, HD, 1),
            lax.dynamic_slice_in_dim(summed, (KVH + my_head) * HD, HD, 1),
        ],
        axis=1,
    ).astype(jnp.bfloat16)
    arrived = lax.all_to_all(sent, "cache", split_axis=1, concat_axis=1, tiled=True)
    arrived = jnp.repeat(arrived, members // KVH, axis=0)
    arrived = lax.all_to_all(arrived, "dev", split_axis=0, concat_axis=0, tiled=True)
    out = plain_attention(
        queries[0], own_self, arrived.reshape(-1, 2 * HD), keep.reshape(-1, HD), redone
    )
    return out[None]


def solution(mesh):
    placed = (
        P("cache", None, "dev"),
        P("cache", "dev", None),
        P("cache", None, None),
        P("cache", None, "dev"),
        P("dev"),
        P("dev", None),
        P(),
        P(),
        P("cache", None, None),
    )
    return jax.shard_map(
        shards, mesh=mesh, in_specs=placed, out_specs=P("cache", None, "dev"), check_vma=False
    )
```
